512 devices in a mesh: row: 32 (over z, x), col: 8 (over y), layer: 2 (over core).
Axes of the slice: x: 4, y: 8, z: 8, core: 2. Of those that a mesh axis runs over, the one named last changes fastest.
Arguments:
- blocks: bfloat16 [1536, 12, 128, 128], P(('row', 'col', 'layer')), may hold values from -0.75 to 0.75
- block_rows: int32 [1536, 12], P(('row', 'col', 'layer')), may hold values from 0 to 1535, as said below
Outputs:
- refined: bfloat16 [1536, 12, 128, 128], P(('row', 'col', 'layer'))
The draws below stay inside these ranges and needn't reach their ends.
Inputs may be any that keep to these rules, and one draw needn't show every extreme that they name: `block_rows`: in block column c the 12 entries are distinct, include c itself, and each equals (c + d) mod 1536 with -8 <= d <= 8.
All inputs are finite; a program needn't handle non-finite values.
Results may differ from the reference program's by a relative error of at most 0.0049.
Values may be sent and summed in bfloat16 or wider, within the bound.
No kernel may reach another device: no remote copies, remote signals or barrier semaphores. Data moves between devices by JAX's collectives and lax.ppermute only.
A program may use at most 64 MiB of HBM per device.

```python
import jax
import jax.numpy as jnp
from jax import lax

TILE = 128
SLOTS = 12
BAND = 8
COLS_DEV = 3
NT = 1536


def draw_block_rows(key, part):
    key = jax.random.fold_in(key, 11)
    first_key, second_key = jax.random.split(key)
    candidates = 2 * BAND + 1
    scores = jax.random.randint(first_key, (NT, candidates), 0, 1 << 20) * candidates + jnp.arange(candidates)
    scores = jnp.where(jnp.arange(candidates)[None, :] == BAND, -1, scores)
    ranked = jnp.argsort(scores, axis=1, stable=True)[:, :SLOTS]
    chosen = (jnp.arange(NT)[:, None] + ranked - BAND) % NT
    mixing = jax.random.randint(second_key, (NT, SLOTS), 0, 1 << 20) * SLOTS + jnp.arange(SLOTS)
    shuffle = jnp.argsort(mixing, axis=1, stable=True)
    return jnp.take_along_axis(chosen, shuffle, axis=1).astype(jnp.int32)


def level_of(own_key, extent, cuts, low, top_value):
    loudness, own = 1.0, jax.random.fold_in(own_key, 6)
    for dim, blocks in cuts:
        draws = jnp.exp(jax.random.uniform(jax.random.fold_in(own, dim), (blocks,), jnp.float32, low / len(cuts), top_value / len(cuts)))
        loudness = loudness * jnp.repeat(draws, extent[dim] // blocks).reshape([-1 if axis == dim else 1 for axis in range(len(extent))])
    return loudness


def noise(own_key, shape, width, most, cuts=(), held_as=jnp.bfloat16):
    entries = width * jax.random.normal(own_key, shape, jnp.float32)
    if cuts:
        entries = entries * level_of(own_key, shape, cuts, -0.22, 0.18)
    return jnp.clip(entries, -most, most).astype(held_as)


def setup_inputs(seed: int = 0) -> dict:
    streams_of = jax.random.split(jax.random.key(seed), 3)
    blocks = noise(streams_of[0], (NT, SLOTS, TILE, TILE), (TILE // 2) ** -0.5, 0.75, ((0, 512),))
    block_rows = draw_block_rows(jax.random.fold_in(streams_of[2], 71), 0)
    return dict(blocks=blocks, block_rows=block_rows)


def select_blocks(blocks, block_rows, columns):
    partners = block_rows[columns]
    their_rows = block_rows[partners]
    matches = their_rows[:, :, :, None] == partners[:, None, None, :]
    slot_ids = jnp.arange(SLOTS, dtype=jnp.int32)[None, None, :, None]
    position = jnp.sum(jnp.where(matches, slot_ids, 0), axis=2).astype(jnp.int32)
    present = jnp.any(matches, axis=2)
    selected = blocks[partners[:, :, None], position]
    return jnp.where(present[..., None, None], selected, jnp.zeros((), selected.dtype))


def multiply(blocks, block_rows, right):
    def one_group(columns):
        selected = select_blocks(blocks, block_rows, columns).astype(jnp.float32)
        return jnp.einsum('basnm,bamq->bsnq', selected, right[columns].astype(jnp.float32))

    groups = jnp.arange(NT, dtype=jnp.int32).reshape(NT // COLS_DEV, COLS_DEV)
    result = lax.map(one_group, groups)
    return result.reshape(NT, SLOTS, TILE, TILE)


def reference(blocks, block_rows):
    square = multiply(blocks, block_rows, blocks).astype(jnp.bfloat16)
    cubed = multiply(blocks, block_rows, square)
    return (3.0 * square.astype(jnp.float32) - 2.0 * cubed).astype(jnp.bfloat16)
```

```python
import jax
import jax.numpy as jnp
from jax import lax
from jax.experimental import pallas as pl
from jax.experimental.pallas import tpu as pltpu
from jax.sharding import PartitionSpec as P

AXES = ("row", "col", "layer")
BAND = 8
TILE = 128
SLOTS = 12
COLS = 3
OWN = COLS * SLOTS
META = 16
BODY = OWN * TILE
FULL = META + BODY + META
FAR = BAND + 1
NEAR = BAND + 2
RELAY = FAR + NEAR
SHARED = 6 * OWN
ZERO = SHARED + RELAY
BLOCKS = ZERO + 1
WIDE = SLOTS * TILE
ANY = pl.BlockSpec(memory_space=pl.ANY)


def send(value, pairs):
    return lax.ppermute(value, AXES, pairs)


def pack_kernel(blocks, meta, out, sem):
    copies = [
        pltpu.make_async_copy(meta, out.at[pl.ds(0, META)], sem.at[0]),
        pltpu.make_async_copy(meta, out.at[pl.ds(META + BODY, META)], sem.at[1]),
    ]
    for c in range(COLS):
        copies.append(
            pltpu.make_async_copy(
                blocks.at[pl.ds(c * WIDE, WIDE)],
                out.at[pl.ds(META + c * WIDE, WIDE)],
                sem.at[2 + c],
            )
        )
    for copy in copies:
        copy.start()
    for copy in copies:
        copy.wait()


def pack(blocks, meta):
    return pl.pallas_call(
        pack_kernel,
        out_shape=jax.ShapeDtypeStruct((FULL, TILE), jnp.bfloat16),
        in_specs=[ANY, ANY],
        out_specs=ANY,
        scratch_shapes=[pltpu.SemaphoreType.DMA((2 + COLS,))],
        cost_estimate=pl.CostEstimate(flops=0, bytes_accessed=4 * BODY * TILE, transcendentals=0),
    )(blocks, meta)


def relay_kernel(index, packed, out, zeros, sem):
    zeros[...] = jnp.zeros_like(zeros)

    def start(i, carry):
        where = index[i]
        target = out.at[pl.ds(pl.multiple_of(i * TILE, TILE), TILE)]

        @pl.when(where < OWN)
        def _():
            source = pl.multiple_of(META + where * TILE, META)
            pltpu.make_async_copy(packed.at[pl.ds(source, TILE)], target, sem).start()

        @pl.when(where >= OWN)
        def _():
            pltpu.make_async_copy(zeros, target, sem).start()

        return carry

    lax.fori_loop(0, RELAY, start, 0)
    pltpu.make_async_copy(out, out, sem).wait()


def relay_blocks(index, packed):
    return pl.pallas_call(
        relay_kernel,
        out_shape=jax.ShapeDtypeStruct((RELAY * TILE, TILE), jnp.bfloat16),
        in_specs=[pl.BlockSpec(memory_space=pltpu.SMEM), ANY],
        out_specs=ANY,
        scratch_shapes=[pltpu.VMEM((TILE, TILE), jnp.bfloat16), pltpu.SemaphoreType.DMA],
        cost_estimate=pl.CostEstimate(
            flops=0, bytes_accessed=4 * RELAY * TILE * TILE, transcendentals=0
        ),
    )(index, packed)


def refine_kernel(index, own, f, g, x0, xf, xg, relay, out, near, left, square, sem):
    copies = [pltpu.make_async_copy(own, near.at[pl.ds(0, BODY)], sem.at[0])]
    for i, packed in enumerate((f, g, x0, xf, xg), 1):
        copies.append(
            pltpu.make_async_copy(
                packed.at[pl.ds(META, BODY)], near.at[pl.ds(i * BODY, BODY)], sem.at[i]
            )
        )
    copies.append(
        pltpu.make_async_copy(
            relay, near.at[pl.ds(SHARED * TILE, RELAY * TILE)], sem.at[6]
        )
    )
    for copy in copies:
        copy.start()
    near[pl.ds(ZERO * TILE, TILE), :] = jnp.zeros((TILE, TILE), jnp.bfloat16)
    for copy in copies:
        copy.wait()
    for c in range(COLS):

        def gather(s, carry):
            for k in range(SLOTS):
                where = index[(c * SLOTS + s) * SLOTS + k]
                left[pl.ds(pl.multiple_of(s * TILE, TILE), TILE), pl.ds(k * TILE, TILE)] = near[
                    pl.ds(pl.multiple_of(where * TILE, TILE), TILE), :
                ]
            return carry

        lax.fori_loop(0, SLOTS, gather, 0)
        square[...] = jnp.dot(
            left[...], near[pl.ds(c * WIDE, WIDE), :], preferred_element_type=jnp.float32
        ).astype(jnp.bfloat16)
        cubed = jnp.dot(left[...], square[...], preferred_element_type=jnp.float32)
        out[pl.ds(c * WIDE, WIDE), :] = (
            3.0 * square[...].astype(jnp.float32) - 2.0 * cubed
        ).astype(jnp.bfloat16)


def refine(index, own, *parts):
    return pl.pallas_call(
        refine_kernel,
        out_shape=jax.ShapeDtypeStruct((BODY, TILE), jnp.bfloat16),
        in_specs=[pl.BlockSpec(memory_space=pltpu.SMEM)] + [ANY] * 7,
        out_specs=pl.BlockSpec(memory_space=pltpu.VMEM),
        scratch_shapes=[
            pltpu.VMEM((BLOCKS * TILE, TILE), jnp.bfloat16),
            pltpu.VMEM((WIDE, WIDE), jnp.bfloat16),
            pltpu.VMEM((WIDE, TILE), jnp.bfloat16),
            pltpu.SemaphoreType.DMA((7,)),
        ],
        compiler_params=pltpu.CompilerParams(vmem_limit_bytes=40 * 2**20),
        cost_estimate=pl.CostEstimate(
            flops=4 * COLS * WIDE * WIDE * TILE, bytes_accessed=2 * BLOCKS * TILE * TILE, transcendentals=0
        ),
    )(index, own, *parts)


def shards(blocks, block_rows):
    count = lax.axis_size(AXES)
    device = lax.axis_index(AXES)
    odd = device % 2
    total = COLS * count
    columns = device * COLS + jnp.arange(COLS, dtype=jnp.int32)
    offsets = (block_rows - columns[:, None] + total // 2) % total - total // 2
    meta = jnp.zeros((META, TILE), jnp.bfloat16).at[:COLS, :SLOTS].set(offsets.astype(jnp.bfloat16))
    own = blocks.reshape(BODY, TILE)
    packed = pack(own, meta)

    devices = range(count)
    outward = [(s, (s + (2 if s % 2 else -2)) % count) for s in devices]
    inward = [(s, (s + (-2 if s % 2 else 2)) % count) for s in devices]
    across = [(s, s ^ 1) for s in devices]
    onward = [(s, (s + (1 if s % 2 else -1)) % count) for s in devices]

    def read_meta(part):
        return part[:COLS, :SLOTS].astype(jnp.int32)

    f = send(packed, outward)
    x0 = send(packed, across)
    g = send(packed, inward)

    far = jnp.arange(FAR, dtype=jnp.int32)
    near = jnp.arange(NEAR, dtype=jnp.int32)
    away = jnp.concatenate([far, near - 1])
    here = jnp.concatenate([far - BAND, near - BAND])
    relay_wanted = jnp.where(odd == 1, away, here)
    relay_column = jnp.where(jnp.arange(RELAY) < FAR, 1, 2 * odd)
    f_meta = read_meta(f)
    f_keys = (f_meta + jnp.arange(COLS, dtype=jnp.int32)[:, None] * 64).reshape(1, OWN)
    hits = (relay_wanted + relay_column * 64)[:, None] == f_keys
    relay_index = jnp.min(
        jnp.where(hits, jnp.arange(OWN, dtype=jnp.int32)[None, :], OWN), axis=1
    )
    relay = send(relay_blocks(relay_index, f), onward)
    xf = send(f, across)
    xg = send(g, across)

    side = 1 - 2 * odd
    local = jnp.arange(COLS, dtype=jnp.int32)[:, None]

    def keys(first, meta):
        column = first + local
        return ((column + meta + 32) * 64 + column + 32).reshape(1, OWN)

    relay_column = jnp.where(
        odd == 1,
        jnp.where(jnp.arange(RELAY) < FAR, 10, 9),
        jnp.where(jnp.arange(RELAY) < FAR, -8, -7),
    )
    relay_offset = jnp.where(odd == 1, here, away)
    all_keys = jnp.concatenate(
        [
            keys(0, offsets),
            keys(6 * side, f_meta),
            keys(-6 * side, read_meta(g)),
            keys(3 * side, read_meta(x0)),
            keys(-3 * side, read_meta(xf)),
            keys(9 * side, read_meta(xg)),
            ((relay_column + relay_offset + 32) * 64 + relay_column + 32).reshape(1, RELAY),
        ],
        axis=1,
    )
    places = local + offsets
    wanted = ((places[:, :, None] + 32) * 64 + places[:, None, :] + 32).reshape(-1, 1)
    index = jnp.min(
        jnp.where(wanted == all_keys, jnp.arange(ZERO, dtype=jnp.int32)[None, :], ZERO), axis=1
    )
    result = refine(index, own, f, g, x0, xf, xg, relay)
    return result.reshape(COLS, SLOTS, TILE, TILE)


def solution(mesh):
    placed = (P(AXES, None, None, None), P(AXES, None))
    return jax.shard_map(
        shards,
        mesh=mesh,
        in_specs=placed,
        out_specs=P(AXES, None, None, None),
        check_vma=False,
    )
```

```python
import functools

import jax
import jax.numpy as jnp
from jax import lax
from jax.experimental import pallas as pl
from jax.experimental.pallas import tpu as pltpu
from jax.sharding import PartitionSpec as P

AXES = ("row", "col", "layer")
BAND = 8
TILE = 128
SLOTS = 12
COLS = 3
OWN = COLS * SLOTS
BODY = OWN * TILE
WIDE = SLOTS * TILE
META = 16
FULL = BODY + META
TALL = WIDE + TILE
FAR = BAND + 1
NEAR = BAND + 2
RELAY = FAR + NEAR
PLACE_AT = 0
ORDER_AT = PLACE_AT + OWN
SLOT_AT = ORDER_AT + OWN
SPAN = 40
SHIFT = 18
FIND_AT = SLOT_AT + OWN
STAGES = 3
TILES_AT = FIND_AT + COLS * SPAN
TABLE = TILES_AT + COLS * STAGES
PAIR = 2 * TILE
PAIRS = SLOTS // 2
CHUNK = 256
BF16 = jnp.bfloat16
F32 = jnp.float32
ANY = pl.BlockSpec(memory_space=pl.ANY)
VMEM = pl.BlockSpec(memory_space=pltpu.VMEM)
SMEM = pl.BlockSpec(memory_space=pltpu.SMEM)


def rows_at(start, size, unit=TILE):
    return pl.ds(pl.multiple_of(start, unit), size)


def call(kernel, out_shape, in_specs, out_specs, scratch, aliases, micros, *args):
    args = [
        pltpu.with_memory_space_constraint(arg, pltpu.VMEM) if spec is VMEM else arg
        for arg, spec in zip(args, in_specs)
    ]
    return pl.pallas_call(
        kernel,
        out_shape=out_shape,
        in_specs=in_specs,
        out_specs=out_specs,
        scratch_shapes=scratch,
        input_output_aliases=aliases,
        compiler_params=pltpu.CompilerParams(vmem_limit_bytes=16 * 2**20),
        cost_estimate=pl.CostEstimate(
            flops=0, bytes_accessed=int(micros * 3e6), transcendentals=0
        ),
    )(*args)


def wrapped(value, total):
    value = jnp.where(value >= total // 2, value - total, value)
    return jnp.where(value < -(total // 2), value + total, value)


def pack_kernel(total, device, rows, mine, packed, wide):
    packed[pl.ds(0, BODY), :] = mine[...]
    column = device[0] * COLS + lax.broadcasted_iota(jnp.int32, (COLS, SLOTS), 0)
    wide[...] = jnp.zeros_like(wide)
    wide[pl.ds(0, COLS), pl.ds(0, SLOTS)] = wrapped(rows[...] - column, total).astype(F32)
    packed[pl.ds(BODY, META), :] = wide[...].astype(BF16)


def table_kernel(total, device, rows, table):
    odd = device[0] % 2
    first = device[0] * COLS
    for c in range(COLS):
        for i in range(SPAN):
            table[FIND_AT + c * SPAN + i] = SLOTS
        places = [wrapped(rows[c, s] - first, total) for s in range(SLOTS)]
        keys, stages = [], []
        for s in range(SLOTS):
            group = (places[s] + BAND + 1) // COLS
            group = jnp.where(odd == 1, 6 - group, group)
            stage = jnp.where(group >= 3, jnp.maximum(group - 4, 0), 3 - group)
            stages.append(stage)
            keys.append(stage * 16 + s)
        for s in range(SLOTS):
            order = jnp.int32(0)
            for other in range(SLOTS):
                if other != s:
                    order = order + jnp.where(keys[other] < keys[s], 1, 0)
            table[PLACE_AT + c * SLOTS + s] = places[s]
            table[ORDER_AT + c * SLOTS + s] = order
            table[SLOT_AT + c * SLOTS + order] = s
            table[FIND_AT + c * SPAN + places[s] + SHIFT] = order
        for stage in range(STAGES):
            held = jnp.int32(0)
            for s in range(SLOTS):
                held = held + jnp.where(stages[s] <= stage, 1, 0)
            table[TILES_AT + c * STAGES + stage] = held // 2


def read_meta(packed, whole, offsets, sem):
    whole[...] = packed[pl.ds(BODY, META), :].astype(F32).astype(jnp.int32)
    copy = pltpu.make_async_copy(whole, offsets, sem)
    copy.start()
    return copy


def scatter(table, left, part, place, offset_at):
    def one(i, carry):
        j = i // COLS
        c = i - j * COLS
        here = FIND_AT + c * SPAN + SHIFT + place + j
        k = table[here]

        @pl.when(k < SLOTS)
        def _():
            for p in range(SLOTS):
                s = table[here + offset_at(j, p)]
                left[
                    rows_at(c * TALL + s * TILE, TILE), rows_at(k * TILE, TILE)
                ] = part[rows_at((j * SLOTS + p) * TILE, TILE), :]

        return carry

    lax.fori_loop(0, COLS * COLS, one, 0)


def accumulate(left, right, total, c, low, high):
    def one(t, carry):
        weights = right[rows_at(c * WIDE + t * PAIR, PAIR), :]
        for m in range(0, WIDE, CHUNK):
            here = rows_at(c * WIDE + m, CHUNK)
            total[here, :] += jnp.dot(
                left[rows_at(c * TALL + m, CHUNK), rows_at(t * PAIR, PAIR, PAIR)],
                weights,
                preferred_element_type=F32,
            )
        return carry

    lax.fori_loop(low, high, one, 0)


def tiles(table, c, stage):
    return table[TILES_AT + c * STAGES + stage]


def finish(table, left, total, c, square, result, out, sem):
    square[...] = total[rows_at(c * WIDE, WIDE), :].astype(BF16)
    for m in range(0, WIDE, CHUNK):
        cubed = jnp.dot(
            left[rows_at(c * TALL + m, CHUNK), :], square[...], preferred_element_type=F32
        )
        refined = (3.0 * square[pl.ds(m, CHUNK), :].astype(F32) - 2.0 * cubed).astype(BF16)
        for i in range(CHUNK // TILE):
            slot = table[SLOT_AT + c * SLOTS + m // TILE + i]
            result[rows_at(slot * TILE, TILE), :] = refined[i * TILE : (i + 1) * TILE]
    copy = pltpu.make_async_copy(result, out.at[rows_at(c * WIDE, WIDE)], sem)
    copy.start()
    return copy


def own_kernel(device, table, mine, x0, left, total, right, whole, offsets, sem):
    side = 1 - 2 * (device[0] % 2)
    copy = read_meta(x0, whole.at[0], offsets.at[0], sem.at[0])

    def clear(i, carry):
        left[rows_at(i * TILE, TILE), :] = jnp.zeros((TILE, WIDE), BF16)
        return carry

    lax.fori_loop(0, COLS * TALL // TILE, clear, 0)
    total[...] = jnp.zeros_like(total)

    def order(i, carry):
        c = i // SLOTS
        right[rows_at(c * WIDE + table[ORDER_AT + i] * TILE, TILE), :] = mine[
            rows_at(i * TILE, TILE), :
        ]
        return carry

    lax.fori_loop(0, OWN, order, 0)
    scatter(table, left, mine, 0, lambda j, p: table[PLACE_AT + j * SLOTS + p] - j)
    copy.wait()
    scatter(table, left, x0, 3 * side, lambda j, p: offsets[0, j, p])
    for c in range(COLS):
        accumulate(left, right, total, c, 0, tiles(table, c, 0))


def outer_kernel(device, table, left_in, total_in, right, f, xf, left, total, whole, offsets, sem):
    del left_in, total_in
    side = 1 - 2 * (device[0] % 2)
    copies = [
        read_meta(part, whole.at[i], offsets.at[i], sem.at[i]) for i, part in enumerate((f, xf))
    ]
    for i, (part, place) in enumerate(((f, 6), (xf, -3))):
        copies[i].wait()
        scatter(table, left, part, place * side, lambda j, p: offsets[i, j, p])
    for c in range(COLS):
        accumulate(left, right, total, c, tiles(table, c, 0), tiles(table, c, 1))


def early_kernel(
    device, table, left_in, total_in, right, g, xg, left, total, out, whole, offsets, square, result, sem
):
    del left_in, total_in
    odd = device[0] % 2
    side = 1 - 2 * odd
    copies = [
        read_meta(part, whole.at[i], offsets.at[i], sem.at[i]) for i, part in enumerate((g, xg))
    ]
    for i, (part, place) in enumerate(((g, -6), (xg, 9))):
        copies[i].wait()
        scatter(table, left, part, place * side, lambda j, p: offsets[i, j, p])
    first = 2 - 2 * odd
    accumulate(left, right, total, first, tiles(table, first, 1), PAIRS)
    copy = finish(table, left, total, first, square, result, out, sem.at[2])
    for c in (1, 2 * odd):
        accumulate(left, right, total, c, tiles(table, c, 1), tiles(table, c, 2))
    copy.wait()


def last_kernel(
    device, table, left_in, total_in, right, relay, out_in, left, total, out, square, result, sem
):
    del left_in, total_in, out_in
    odd = device[0] % 2
    copies = []
    for i, c in enumerate((1, 2 * odd)):
        for start, size, place, low in (
            (0, FAR, jnp.where(odd == 1, 10, -8), jnp.where(odd == 1, -8, 0)),
            (FAR, NEAR, jnp.where(odd == 1, 9, -7), jnp.where(odd == 1, -8, -1)),
        ):
            here = FIND_AT + c * SPAN + SHIFT + place
            k = table[here]

            @pl.when(k < SLOTS)
            def _():
                for p in range(size):
                    s = table[here + low + p]
                    left[
                        rows_at(c * TALL + s * TILE, TILE), rows_at(k * TILE, TILE)
                    ] = relay[pl.ds((start + p) * TILE, TILE), :]

        accumulate(left, right, total, c, tiles(table, c, 2), PAIRS)
        copies.append(finish(table, left, total, c, square, result.at[i], out, sem.at[i]))
    for copy in copies:
        copy.wait()


def relay_kernel(device, f, relay, whole, offsets, sem):
    odd = device[0] % 2
    copy = read_meta(f, whole, offsets, sem)
    relay[...] = jnp.zeros_like(relay)
    copy.wait()
    for column, start, size, shift in (
        (1, 0, FAR, jnp.where(odd == 1, 0, BAND)),
        (2 * odd, FAR, NEAR, jnp.where(odd == 1, 1, BAND)),
    ):

        def one(p, carry):
            at = offsets[column, p] + shift

            @pl.when((at >= 0) & (at < size))
            def _():
                relay[rows_at((start + at) * TILE, TILE), :] = f[
                    rows_at((column * SLOTS + p) * TILE, TILE), :
                ]

            return carry

        lax.fori_loop(0, SLOTS, one, 0)


def send(value, pairs):
    return lax.ppermute(value, AXES, pairs)


def after(*values):
    return lax.optimization_barrier(values)


def meta_scratch(count):
    return [
        pltpu.VMEM((count, META, TILE), jnp.int32),
        pltpu.SMEM((count, META, TILE), jnp.int32),
    ]


def shards(blocks, block_rows):
    count = lax.axis_size(AXES)
    device = lax.axis_index(AXES)
    columns = COLS * count
    devices = range(count)
    outward = [(s, (s + (2 if s % 2 else -2)) % count) for s in devices]
    inward = [(s, (s + (-2 if s % 2 else 2)) % count) for s in devices]
    onward = [(s, (s + (1 if s % 2 else -1)) % count) for s in devices]
    across = [(s, s ^ 1) for s in devices]

    mine = blocks.reshape(BODY, TILE)
    device = device.astype(jnp.int32).reshape(1)
    packed = call(
        functools.partial(pack_kernel, columns),
        pltpu.VMEM((FULL, TILE), BF16),
        [SMEM, VMEM, VMEM],
        VMEM,
        [pltpu.VMEM((META, TILE), F32)],
        {},
        1,
        device,
        block_rows,
        mine,
    )
    f = send(packed, outward)
    x0 = send(packed, across)
    packed, x0 = after(packed, x0)
    g = send(packed, inward)

    table = call(
        functools.partial(table_kernel, columns),
        jax.ShapeDtypeStruct((TABLE,), jnp.int32),
        [SMEM, SMEM],
        SMEM,
        [],
        {},
        2,
        device,
        block_rows,
    )
    left_shape = pltpu.VMEM((COLS * TALL, WIDE), BF16)
    total_shape = pltpu.VMEM((BODY, TILE), F32)
    out_shape = jax.ShapeDtypeStruct((BODY, TILE), BF16)
    left, total, right = call(
        own_kernel,
        (left_shape, total_shape, pltpu.VMEM((BODY, TILE), BF16)),
        [SMEM, SMEM, VMEM, VMEM],
        (VMEM, VMEM, VMEM),
        [*meta_scratch(1), pltpu.SemaphoreType.DMA((1,))],
        {},
        6,
        device,
        table,
        mine,
        x0,
    )

    f, left = after(f, left)
    relay = call(
        relay_kernel,
        pltpu.VMEM((RELAY * TILE, TILE), BF16),
        [SMEM, VMEM],
        VMEM,
        [
            pltpu.VMEM((META, TILE), jnp.int32),
            pltpu.SMEM((META, TILE), jnp.int32),
            pltpu.SemaphoreType.DMA,
        ],
        {},
        1,
        device,
        f,
    )
    f, relay = after(f, relay)
    relay = send(relay, onward)
    xf = send(f, across)
    xg = send(g, across)
    xf, g = after(xf, g)
    left, total = call(
        outer_kernel,
        (left_shape, total_shape),
        [SMEM, SMEM] + [VMEM] * 5,
        (VMEM, VMEM),
        [*meta_scratch(2), pltpu.SemaphoreType.DMA((2,))],
        {2: 0, 3: 1},
        4,
        device,
        table,
        left,
        total,
        right,
        f,
        xf,
    )
    left, total, out = call(
        early_kernel,
        (left_shape, total_shape, out_shape),
        [SMEM, SMEM] + [VMEM] * 5,
        (VMEM, VMEM, ANY),
        [
            *meta_scratch(2),
            pltpu.VMEM((WIDE, TILE), BF16),
            pltpu.VMEM((WIDE, TILE), BF16),
            pltpu.SemaphoreType.DMA((3,)),
        ],
        {2: 0, 3: 1},
        4,
        device,
        table,
        left,
        total,
        right,
        g,
        xg,
    )
    out = call(
        last_kernel,
        (left_shape, total_shape, out_shape),
        [SMEM, SMEM] + [VMEM] * 4 + [ANY],
        (VMEM, VMEM, ANY),
        [
            pltpu.VMEM((WIDE, TILE), BF16),
            pltpu.VMEM((2, WIDE, TILE), BF16),
            pltpu.SemaphoreType.DMA((2,)),
        ],
        {2: 0, 3: 1, 6: 2},
        4,
        device,
        table,
        left,
        total,
        right,
        relay,
        out,
    )[2]
    return out.reshape(COLS, SLOTS, TILE, TILE)


def solution(mesh):
    placed = (P(AXES, None, None, None), P(AXES, None))
    return jax.shard_map(
        shards,
        mesh=mesh,
        in_specs=placed,
        out_specs=P(AXES, None, None, None),
        check_vma=False,
    )
```

```python
import functools

import jax
import jax.numpy as jnp
from jax import lax
from jax.experimental import pallas as pl
from jax.experimental.pallas import tpu as pltpu
from jax.sharding import PartitionSpec as P

AXES = ("row", "col", "layer")
BAND = 8
TILE = 128
SLOTS = 12
COLS = 3
OWN = COLS * SLOTS
BODY = OWN * TILE
WIDE = SLOTS * TILE
META = 16
FULL = BODY + META
LONG = FULL + META
TALL = WIDE + TILE
FAR = BAND + 1
NEAR = BAND + 2
RELAY = FAR + NEAR
PLACE_AT = 0
ORDER_AT = PLACE_AT + OWN
SLOT_AT = ORDER_AT + OWN
SPAN = 40
SHIFT = 18
FIND_AT = SLOT_AT + OWN
STAGES = 3
TILES_AT = FIND_AT + COLS * SPAN
ODD_AT = TILES_AT + COLS * STAGES
TABLE = ODD_AT + 1
PAIR = 2 * TILE
PAIRS = SLOTS // 2
CHUNK = 256
GROUP = 4
BF16 = jnp.bfloat16
F32 = jnp.float32
ANY = pl.BlockSpec(memory_space=pl.ANY)
VMEM = pl.BlockSpec(memory_space=pltpu.VMEM)
HBM = pl.BlockSpec(memory_space=pltpu.HBM)
SMEM = pl.BlockSpec(memory_space=pltpu.SMEM)


def rows_at(start, size, unit=TILE):
    return pl.ds(pl.multiple_of(start, unit), size)


def call(kernel, out_shape, in_specs, out_specs, scratch, aliases, micros, *args):
    args = [
        pltpu.with_memory_space_constraint(arg, spec.memory_space) if spec in (VMEM, HBM) else arg
        for arg, spec in zip(args, in_specs)
    ]
    return pl.pallas_call(
        kernel,
        out_shape=out_shape,
        in_specs=in_specs,
        out_specs=out_specs,
        scratch_shapes=scratch,
        input_output_aliases=aliases,
        compiler_params=pltpu.CompilerParams(vmem_limit_bytes=16 * 2**20),
        cost_estimate=pl.CostEstimate(
            flops=0, bytes_accessed=int(micros * 3e6), transcendentals=0
        ),
    )(*args)


def wrapped(value, total):
    value = jnp.where(value >= total // 2, value - total, value)
    return jnp.where(value < -(total // 2), value + total, value)


def pack_kernel(total, device, rows, mine, packed, longer, near_rows, wide, sem):
    copies = [
        pltpu.make_async_copy(rows, near_rows, sem.at[0]),
        pltpu.make_async_copy(mine, longer.at[pl.ds(0, BODY)], sem.at[1]),
        pltpu.make_async_copy(mine, packed.at[pl.ds(0, BODY)], sem.at[2]),
    ]
    for copy in copies:
        copy.start()
    column = device[0] * COLS + lax.broadcasted_iota(jnp.int32, (COLS, SLOTS), 0)
    wide[...] = jnp.zeros_like(wide)
    copies[0].wait()
    wide[pl.ds(0, COLS), pl.ds(0, SLOTS)] = wrapped(near_rows[...] - column, total).astype(F32)
    packed[pl.ds(BODY, META), :] = wide[...].astype(BF16)
    longer[pl.ds(BODY, META), :] = wide[...].astype(BF16)
    longer[pl.ds(FULL, META), :] = jnp.zeros((META, TILE), BF16)
    copies[1].wait()
    copies[2].wait()


def table_kernel(total, device, rows, table):
    odd = device[0] % 2
    table[ODD_AT] = odd
    first = device[0] * COLS
    for c in range(COLS):
        for i in range(SPAN):
            table[FIND_AT + c * SPAN + i] = SLOTS
        places = [wrapped(rows[c, s] - first, total) for s in range(SLOTS)]
        keys, stages = [], []
        for s in range(SLOTS):
            group = (places[s] + BAND + 1) // COLS
            group = jnp.where(odd == 1, 6 - group, group)
            stage = jnp.where(group >= 3, jnp.maximum(group - 4, 0), group)
            stage = jnp.where(group == 0, 3, stage)
            stages.append(stage)
            keys.append(stage * 16 + s)
        for s in range(SLOTS):
            order = jnp.int32(0)
            for other in range(SLOTS):
                if other != s:
                    order = order + jnp.where(keys[other] < keys[s], 1, 0)
            table[PLACE_AT + c * SLOTS + s] = places[s]
            table[ORDER_AT + c * SLOTS + s] = order
            table[SLOT_AT + c * SLOTS + order] = s
            table[FIND_AT + c * SPAN + places[s] + SHIFT] = order
        for stage in range(STAGES):
            held = jnp.int32(0)
            for s in range(SLOTS):
                held = held + jnp.where(stages[s] <= stage, 1, 0)
            table[TILES_AT + c * STAGES + stage] = held // 2


def read_meta(packed, whole, offsets, sem):
    whole[...] = packed[pl.ds(BODY, META), :].astype(F32).astype(jnp.int32)
    copy = pltpu.make_async_copy(whole, offsets, sem)
    copy.start()
    return copy


def scatter(table, left, part, place, offset_at):
    for j in range(part.shape[0] // WIDE):
        for c in range(COLS):
            here = FIND_AT + c * SPAN + SHIFT + place + j
            k = table[here]

            @pl.when(k < SLOTS)
            def _():
                for start in range(0, SLOTS, GROUP):
                    taken = range(start, start + GROUP)
                    to = [table[here + offset_at(j, p)] for p in taken]
                    held = [part[rows_at((j * SLOTS + p) * TILE, TILE), :] for p in taken]
                    for s, block in zip(to, held):
                        left[
                            rows_at(c * TALL + s * TILE, TILE), rows_at(k * TILE, TILE)
                        ] = block


def accumulate(left, right, total, c, low, high):
    def one(t, carry):
        weights = right[rows_at(c * WIDE + t * PAIR, PAIR), :]
        for m in range(0, WIDE, CHUNK):
            here = rows_at(c * WIDE + m, CHUNK)
            total[here, :] += jnp.dot(
                left[rows_at(c * TALL + m, CHUNK), rows_at(t * PAIR, PAIR, PAIR)],
                weights,
                preferred_element_type=F32,
            )
        return carry

    lax.fori_loop(low, high, one, 0)


def tiles(table, c, stage):
    return table[TILES_AT + c * STAGES + stage]


def finish(table, left, total, c, square, result, out, sem):
    square[...] = total[rows_at(c * WIDE, WIDE), :].astype(BF16)
    for m in range(0, WIDE, CHUNK):
        cubed = jnp.dot(
            left[rows_at(c * TALL + m, CHUNK), :], square[...], preferred_element_type=F32
        )
        refined = (3.0 * square[pl.ds(m, CHUNK), :].astype(F32) - 2.0 * cubed).astype(BF16)
        for i in range(CHUNK // TILE):
            slot = table[SLOT_AT + c * SLOTS + m // TILE + i]
            here = rows_at(slot * TILE, TILE)
            result[here, :] = refined[i * TILE : (i + 1) * TILE]
            target = out.at[rows_at(c * WIDE + slot * TILE, TILE)]
            pltpu.make_async_copy(result.at[here], target, sem).start()
    return pltpu.make_async_copy(result, out.at[rows_at(c * WIDE, WIDE)], sem)


def own_kernel(table, mine, left, total, right):
    def clear(i, carry):
        left[rows_at(i * TILE, TILE), :] = jnp.zeros((TILE, WIDE), BF16)
        return carry

    lax.fori_loop(0, COLS * TALL // TILE, clear, 0)
    total[...] = jnp.zeros_like(total)

    def order(i, carry):
        c = i // SLOTS
        right[rows_at(c * WIDE + table[ORDER_AT + i] * TILE, TILE), :] = mine[
            rows_at(i * TILE, TILE), :
        ]
        return carry

    lax.fori_loop(0, OWN, order, 0)
    scatter(table, left, mine, 0, lambda j, p: table[PLACE_AT + j * SLOTS + p] - j)


def parts_kernel(places, low, high, table, left_in, total_in, right, *refs):
    del left_in, total_in
    parts, (left, total, whole, offsets, sem) = refs[: len(places)], refs[len(places) :]
    side = 1 - 2 * table[ODD_AT]
    copies = [
        read_meta(part, whole.at[i], offsets.at[i], sem.at[i]) for i, part in enumerate(parts)
    ]
    for i, (part, place) in enumerate(zip(parts, places)):
        copies[i].wait()
        scatter(table, left, part, place * side, lambda j, p: offsets[i, j, p])
    for c in range(COLS):
        accumulate(
            left, right, total, c, 0 if low is None else tiles(table, c, low), tiles(table, c, high)
        )


def add_parts(table, left, total, right, parts, places, low, high, micros):
    count = len(parts)
    return call(
        functools.partial(parts_kernel, places, low, high),
        (pltpu.VMEM(left.shape, BF16), pltpu.VMEM(total.shape, F32)),
        [SMEM] + [VMEM] * (3 + count),
        (VMEM, VMEM),
        [*meta_scratch(count), pltpu.SemaphoreType.DMA((count,))],
        {1: 0, 2: 1},
        micros,
        table,
        left,
        total,
        right,
        *parts,
    )


def early_kernel(
    table, left_in, total_in, right, x, left, total, out, whole, offsets, square, result, sem
):
    del left_in, total_in
    odd = table[ODD_AT]
    side = 1 - 2 * odd
    parts = [x.at[pl.ds(i * LONG, LONG)] for i in range(2)]
    copies = [
        read_meta(part, whole.at[i], offsets.at[i], sem.at[i]) for i, part in enumerate(parts)
    ]
    for i, (part, place) in enumerate(zip(parts, (-3, 9))):
        copies[i].wait()
        scatter(table, left, part, place * side, lambda j, p: offsets[i, j, p])
    first = 2 - 2 * odd
    accumulate(left, right, total, first, tiles(table, first, 1), PAIRS)
    copy = finish(table, left, total, first, square, result, out, sem.at[2])
    for c in (1, 2 * odd):
        accumulate(left, right, total, c, tiles(table, c, 1), tiles(table, c, 2))
    copy.wait()


def last_kernel(
    table, left_in, total_in, right, relay, out_in, left, total, out, square, result, sem
):
    del left_in, total_in, out_in
    odd = table[ODD_AT]
    copies = []
    for i, c in enumerate((1, 2 * odd)):
        for start, size, place, low in (
            (0, FAR, jnp.where(odd == 1, 10, -8), jnp.where(odd == 1, -8, 0)),
            (FAR, NEAR, jnp.where(odd == 1, 9, -7), jnp.where(odd == 1, -8, -1)),
        ):
            here = FIND_AT + c * SPAN + SHIFT + place
            k = table[here]

            @pl.when(k < SLOTS)
            def _():
                for p in range(size):
                    s = table[here + low + p]
                    left[
                        rows_at(c * TALL + s * TILE, TILE), rows_at(k * TILE, TILE)
                    ] = relay[pl.ds((start + p) * TILE, TILE), :]

        accumulate(left, right, total, c, tiles(table, c, 2), PAIRS)
        copies.append(finish(table, left, total, c, square, result.at[i], out, sem.at[i]))
    for copy in copies:
        copy.wait()


def relay_kernel(table, f, g, relay, joined, whole, offsets, sem):
    odd = table[ODD_AT]
    copy = read_meta(f, whole, offsets, sem.at[0])
    joins = [
        pltpu.make_async_copy(part, joined.at[pl.ds(i * LONG, LONG)], sem.at[1 + i])
        for i, part in enumerate((f, g))
    ]
    for join in joins:
        join.start()
    relay[...] = jnp.zeros_like(relay)
    copy.wait()
    for column, start, size, shift in (
        (1, 0, FAR, jnp.where(odd == 1, 0, BAND)),
        (2 * odd, FAR, NEAR, jnp.where(odd == 1, 1, BAND)),
    ):

        def one(p, carry):
            at = offsets[column, p] + shift

            @pl.when((at >= 0) & (at < size))
            def _():
                relay[rows_at((start + at) * TILE, TILE), :] = f[
                    rows_at((column * SLOTS + p) * TILE, TILE), :
                ]

            return carry

        lax.fori_loop(0, SLOTS, one, 0)
    for join in joins:
        join.wait()


def send(value, pairs):
    return lax.ppermute(value, AXES, pairs)


def after(*values):
    return lax.optimization_barrier(values)


def meta_scratch(count):
    return [
        pltpu.VMEM((count, META, TILE), jnp.int32),
        pltpu.SMEM((count, META, TILE), jnp.int32),
    ]


def shards(blocks, block_rows):
    count = lax.axis_size(AXES)
    device = lax.axis_index(AXES)
    columns = COLS * count
    devices = range(count)
    outward = [(s, (s + (2 if s % 2 else -2)) % count) for s in devices]
    inward = [(s, (s + (-2 if s % 2 else 2)) % count) for s in devices]
    onward = [(s, (s + (1 if s % 2 else -1)) % count) for s in devices]
    across = [(s, s ^ 1) for s in devices]

    mine = blocks.reshape(BODY, TILE)
    device = device.astype(jnp.int32).reshape(1)
    packed, longer = call(
        functools.partial(pack_kernel, columns),
        (pltpu.VMEM((FULL, TILE), BF16), pltpu.VMEM((LONG, TILE), BF16)),
        [SMEM, HBM, HBM],
        (VMEM, VMEM),
        [
            pltpu.VMEM((COLS, SLOTS), jnp.int32),
            pltpu.VMEM((META, TILE), F32),
            pltpu.SemaphoreType.DMA((3,)),
        ],
        {},
        1,
        device,
        block_rows,
        mine,
    )
    x0 = send(packed, across)
    f = send(longer, outward)
    g = send(longer, inward)
    table = call(
        functools.partial(table_kernel, columns),
        jax.ShapeDtypeStruct((TABLE,), jnp.int32),
        [SMEM, SMEM],
        SMEM,
        [],
        {},
        2,
        device,
        block_rows,
    )
    left_shape = pltpu.VMEM((COLS * TALL, WIDE), BF16)
    total_shape = pltpu.VMEM((BODY, TILE), F32)
    out_shape = jax.ShapeDtypeStruct((BODY, TILE), BF16)
    left, total, right = call(
        own_kernel,
        (left_shape, total_shape, pltpu.VMEM((BODY, TILE), BF16)),
        [SMEM, VMEM],
        (VMEM, VMEM, VMEM),
        [],
        {},
        8,
        table,
        packed,
    )
    left, total = add_parts(table, left, total, right, (x0,), (3,), None, 0, 4)
    f, left = after(f, left)
    relay, joined = call(
        relay_kernel,
        (pltpu.VMEM((RELAY * TILE, TILE), BF16), pltpu.VMEM((2 * LONG, TILE), BF16)),
        [SMEM, VMEM, VMEM],
        (VMEM, VMEM),
        [
            pltpu.VMEM((META, TILE), jnp.int32),
            pltpu.SMEM((META, TILE), jnp.int32),
            pltpu.SemaphoreType.DMA((3,)),
        ],
        {},
        1,
        table,
        f,
        g,
    )
    relay = send(relay, onward)
    x = send(joined, across)
    left, total = add_parts(table, left, total, right, (f, g), (6, -6), 0, 1, 4)
    x, left = after(x, left)
    left, total, out = call(
        early_kernel,
        (left_shape, total_shape, out_shape),
        [SMEM] + [VMEM] * 4,
        (VMEM, VMEM, ANY),
        [
            *meta_scratch(2),
            pltpu.VMEM((WIDE, TILE), BF16),
            pltpu.VMEM((WIDE, TILE), BF16),
            pltpu.SemaphoreType.DMA((3,)),
        ],
        {1: 0, 2: 1},
        4,
        table,
        left,
        total,
        right,
        x,
    )
    out = call(
        last_kernel,
        (left_shape, total_shape, out_shape),
        [SMEM] + [VMEM] * 4 + [ANY],
        (VMEM, VMEM, ANY),
        [
            pltpu.VMEM((WIDE, TILE), BF16),
            pltpu.VMEM((2, WIDE, TILE), BF16),
            pltpu.SemaphoreType.DMA((2,)),
        ],
        {1: 0, 2: 1, 5: 2},
        4,
        table,
        left,
        total,
        right,
        relay,
        out,
    )[2]
    return out.reshape(COLS, SLOTS, TILE, TILE)


def solution(mesh):
    placed = (P(AXES, None, None, None), P(AXES, None))
    return jax.shard_map(
        shards,
        mesh=mesh,
        in_specs=placed,
        out_specs=P(AXES, None, None, None),
        check_vma=False,
    )
```

```python
import functools

import jax
import jax.numpy as jnp
from jax import lax
from jax.experimental import pallas as pl
from jax.experimental.pallas import tpu as pltpu
from jax.sharding import PartitionSpec as P

AXES = ("row", "col", "layer")
BAND = 8
TILE = 128
SLOTS = 12
COLS = 3
OWN = COLS * SLOTS
BODY = OWN * TILE
WIDE = SLOTS * TILE
META = 16
FULL = BODY + META
LONG = FULL + META
TALL = WIDE + TILE
FAR = BAND + 1
NEAR = BAND + 2
RELAY = FAR + NEAR
PLACE_AT = 0
ORDER_AT = PLACE_AT + OWN
SLOT_AT = ORDER_AT + OWN
SPAN = 40
SHIFT = 18
FIND_AT = SLOT_AT + OWN
STAGES = 3
TILES_AT = FIND_AT + COLS * SPAN
ODD_AT = TILES_AT + COLS * STAGES
TABLE = ODD_AT + 1
PAIR = 2 * TILE
PAIRS = SLOTS // 2
CHUNK = 256
GROUP = 4
BF16 = jnp.bfloat16
F32 = jnp.float32
ANY = pl.BlockSpec(memory_space=pl.ANY)
VMEM = pl.BlockSpec(memory_space=pltpu.VMEM)
HBM = pl.BlockSpec(memory_space=pltpu.HBM)
SMEM = pl.BlockSpec(memory_space=pltpu.SMEM)


def rows_at(start, size, unit=TILE):
    return pl.ds(pl.multiple_of(start, unit), size)


def call(kernel, out_shape, in_specs, out_specs, scratch, aliases, micros, *args):
    args = [
        pltpu.with_memory_space_constraint(arg, spec.memory_space) if spec in (VMEM, HBM) else arg
        for arg, spec in zip(args, in_specs)
    ]
    return pl.pallas_call(
        kernel,
        out_shape=out_shape,
        in_specs=in_specs,
        out_specs=out_specs,
        scratch_shapes=scratch,
        input_output_aliases=aliases,
        compiler_params=pltpu.CompilerParams(vmem_limit_bytes=16 * 2**20),
        cost_estimate=pl.CostEstimate(
            flops=0, bytes_accessed=int(micros * 3e6), transcendentals=0
        ),
    )(*args)


def wrapped(value, total):
    value = jnp.where(value >= total // 2, value - total, value)
    return jnp.where(value < -(total // 2), value + total, value)


def pack_kernel(total, device, rows, mine, longer, near_rows, wide, sem):
    body = pltpu.make_async_copy(mine, longer.at[pl.ds(0, BODY)], sem.at[0])
    lists = pltpu.make_async_copy(rows, near_rows, sem.at[1])
    body.start()
    lists.start()
    column = device[0] * COLS + lax.broadcasted_iota(jnp.int32, (COLS, SLOTS), 0)
    wide[...] = jnp.zeros_like(wide)
    longer[pl.ds(FULL, META), :] = jnp.zeros((META, TILE), BF16)
    lists.wait()
    wide[pl.ds(0, COLS), pl.ds(0, SLOTS)] = wrapped(near_rows[...] - column, total).astype(F32)
    longer[pl.ds(BODY, META), :] = wide[...].astype(BF16)
    body.wait()


def shorten_kernel(longer, packed, sem):
    copy = pltpu.make_async_copy(longer.at[pl.ds(0, FULL)], packed, sem)
    copy.start()
    copy.wait()


def table_kernel(total, device, rows, table):
    odd = device[0] % 2
    table[ODD_AT] = odd
    first = device[0] * COLS
    for c in range(COLS):
        for i in range(SPAN):
            table[FIND_AT + c * SPAN + i] = SLOTS
        places = [wrapped(rows[c, s] - first, total) for s in range(SLOTS)]
        keys, stages = [], []
        for s in range(SLOTS):
            group = (places[s] + BAND + 1) // COLS
            group = jnp.where(odd == 1, 6 - group, group)
            stage = jnp.where(group >= 3, jnp.maximum(group - 4, 0), group)
            stage = jnp.where(group == 0, 3, stage)
            stages.append(stage)
            keys.append(stage * 16 + s)
        for s in range(SLOTS):
            order = jnp.int32(0)
            for other in range(SLOTS):
                if other != s:
                    order = order + jnp.where(keys[other] < keys[s], 1, 0)
            table[PLACE_AT + c * SLOTS + s] = places[s]
            table[ORDER_AT + c * SLOTS + s] = order
            table[SLOT_AT + c * SLOTS + order] = s
            table[FIND_AT + c * SPAN + places[s] + SHIFT] = order
        for stage in range(STAGES):
            held = jnp.int32(0)
            for s in range(SLOTS):
                held = held + jnp.where(stages[s] <= stage, 1, 0)
            table[TILES_AT + c * STAGES + stage] = held // 2


def read_meta(packed, whole, offsets, sem):
    whole[...] = packed[pl.ds(BODY, META), :].astype(F32).astype(jnp.int32)
    copy = pltpu.make_async_copy(whole, offsets, sem)
    copy.start()
    return copy


def scatter(table, left, part, place, offset_at):
    for j in range(part.shape[0] // WIDE):
        for c in range(COLS):
            here = FIND_AT + c * SPAN + SHIFT + place + j
            k = table[here]

            @pl.when(k < SLOTS)
            def _():
                for start in range(0, SLOTS, GROUP):
                    taken = range(start, start + GROUP)
                    to = [table[here + offset_at(j, p)] for p in taken]
                    held = [part[rows_at((j * SLOTS + p) * TILE, TILE), :] for p in taken]
                    for s, block in zip(to, held):
                        left[
                            rows_at(c * TALL + s * TILE, TILE), rows_at(k * TILE, TILE)
                        ] = block


def accumulate(left, right, total, c, low, high):
    def one(t, carry):
        weights = right[rows_at(c * WIDE + t * PAIR, PAIR), :]
        for m in range(0, WIDE, CHUNK):
            here = rows_at(c * WIDE + m, CHUNK)
            total[here, :] += jnp.dot(
                left[rows_at(c * TALL + m, CHUNK), rows_at(t * PAIR, PAIR, PAIR)],
                weights,
                preferred_element_type=F32,
            )
        return carry

    lax.fori_loop(low, high, one, 0)


def tiles(table, c, stage):
    return table[TILES_AT + c * STAGES + stage]


def finish(table, left, total, c, square, result, out, sem):
    square[...] = total[rows_at(c * WIDE, WIDE), :].astype(BF16)
    for m in range(0, WIDE, CHUNK):
        cubed = jnp.dot(
            left[rows_at(c * TALL + m, CHUNK), :], square[...], preferred_element_type=F32
        )
        refined = (3.0 * square[pl.ds(m, CHUNK), :].astype(F32) - 2.0 * cubed).astype(BF16)
        for i in range(CHUNK // TILE):
            slot = table[SLOT_AT + c * SLOTS + m // TILE + i]
            here = rows_at(slot * TILE, TILE)
            result[here, :] = refined[i * TILE : (i + 1) * TILE]
            target = out.at[rows_at(c * WIDE + slot * TILE, TILE)]
            pltpu.make_async_copy(result.at[here], target, sem).start()
    return pltpu.make_async_copy(result, out.at[rows_at(c * WIDE, WIDE)], sem)


def own_kernel(table, mine, left, total, right):
    def clear(i, carry):
        left[rows_at(i * TILE, TILE), :] = jnp.zeros((TILE, WIDE), BF16)
        return carry

    lax.fori_loop(0, COLS * TALL // TILE, clear, 0)
    total[...] = jnp.zeros_like(total)

    def order(i, carry):
        c = i // SLOTS
        right[rows_at(c * WIDE + table[ORDER_AT + i] * TILE, TILE), :] = mine[
            rows_at(i * TILE, TILE), :
        ]
        return carry

    lax.fori_loop(0, OWN, order, 0)
    scatter(table, left, mine, 0, lambda j, p: table[PLACE_AT + j * SLOTS + p] - j)


def parts_kernel(places, low, high, table, left_in, total_in, right, *refs):
    del left_in, total_in
    parts, (left, total, whole, offsets, sem) = refs[: len(places)], refs[len(places) :]
    side = 1 - 2 * table[ODD_AT]
    copies = [
        read_meta(part, whole.at[i], offsets.at[i], sem.at[i]) for i, part in enumerate(parts)
    ]
    for i, (part, place) in enumerate(zip(parts, places)):
        copies[i].wait()
        scatter(table, left, part, place * side, lambda j, p: offsets[i, j, p])
    for c in range(COLS):
        accumulate(
            left, right, total, c, 0 if low is None else tiles(table, c, low), tiles(table, c, high)
        )


def add_parts(table, left, total, right, parts, places, low, high, micros):
    count = len(parts)
    return call(
        functools.partial(parts_kernel, places, low, high),
        (pltpu.VMEM(left.shape, BF16), pltpu.VMEM(total.shape, F32)),
        [SMEM] + [VMEM] * (3 + count),
        (VMEM, VMEM),
        [*meta_scratch(count), pltpu.SemaphoreType.DMA((count,))],
        {1: 0, 2: 1},
        micros,
        table,
        left,
        total,
        right,
        *parts,
    )


def early_kernel(
    table, left_in, total_in, right, x, left, total, out, whole, offsets, square, result, sem
):
    del left_in, total_in
    odd = table[ODD_AT]
    side = 1 - 2 * odd
    parts = [x.at[pl.ds(i * LONG, LONG)] for i in range(2)]
    copies = [
        read_meta(part, whole.at[i], offsets.at[i], sem.at[i]) for i, part in enumerate(parts)
    ]
    for c in range(COLS):
        accumulate(left, right, total, c, tiles(table, c, 0), tiles(table, c, 1))
    for i, (part, place) in enumerate(zip(parts, (-3, 9))):
        copies[i].wait()
        scatter(table, left, part, place * side, lambda j, p: offsets[i, j, p])
    first = 2 - 2 * odd
    accumulate(left, right, total, first, tiles(table, first, 1), PAIRS)
    copy = finish(table, left, total, first, square, result, out, sem.at[2])
    for c in (1, 2 * odd):
        accumulate(left, right, total, c, tiles(table, c, 1), tiles(table, c, 2))
    copy.wait()


def last_kernel(
    table, left_in, total_in, right, relay, out_in, left, total, out, square, result, sem
):
    del left_in, total_in, out_in
    odd = table[ODD_AT]
    copies = []
    for i, c in enumerate((1, 2 * odd)):
        for start, size, place, low in (
            (0, FAR, jnp.where(odd == 1, 10, -8), jnp.where(odd == 1, -8, 0)),
            (FAR, NEAR, jnp.where(odd == 1, 9, -7), jnp.where(odd == 1, -8, -1)),
        ):
            here = FIND_AT + c * SPAN + SHIFT + place
            k = table[here]

            @pl.when(k < SLOTS)
            def _():
                for p in range(size):
                    s = table[here + low + p]
                    left[
                        rows_at(c * TALL + s * TILE, TILE), rows_at(k * TILE, TILE)
                    ] = relay[pl.ds((start + p) * TILE, TILE), :]

        accumulate(left, right, total, c, tiles(table, c, 2), PAIRS)
        copies.append(finish(table, left, total, c, square, result.at[i], out, sem.at[i]))
    for copy in copies:
        copy.wait()


def fill_relay(odd, f, relay, offsets):
    relay[...] = jnp.zeros_like(relay)
    for column, start, size, shift in (
        (1, 0, FAR, 0 if odd else BAND),
        (2 * odd, FAR, NEAR, 1 if odd else BAND),
    ):

        def one(p, carry):
            at = offsets[column, p] + shift

            @pl.when((at >= 0) & (at < size))
            def _():
                relay[rows_at((start + at) * TILE, TILE), :] = f[
                    rows_at((column * SLOTS + p) * TILE, TILE), :
                ]

            return carry

        lax.fori_loop(0, SLOTS, one, 0)


def odd_kernel(table, f, left_in, relay, left, whole, offsets, sem):
    del left_in

    @pl.when(table[ODD_AT] == 1)
    def _():
        read_meta(f, whole, offsets, sem).wait()
        fill_relay(1, f, relay, offsets)
        scatter(table, left, f, -6, lambda j, p: offsets[j, p])


def even_kernel(device, f, relay_in, relay, whole, offsets, sem):
    del relay_in

    @pl.when(device[0] % 2 == 0)
    def _():
        read_meta(f, whole, offsets, sem).wait()
        fill_relay(0, f, relay, offsets)


def join_kernel(f, g, joined, sem):
    joins = [
        pltpu.make_async_copy(part, joined.at[pl.ds(i * LONG, LONG)], sem.at[i])
        for i, part in enumerate((f, g))
    ]
    for join in joins:
        join.start()
    for join in joins:
        join.wait()


def near_kernel(table, left_in, f, g, left, whole, offsets, sem):
    del left_in
    odd = table[ODD_AT]
    copies = [
        read_meta(part, whole.at[i], offsets.at[i], sem.at[i]) for i, part in enumerate((g, f))
    ]
    for copy in copies:
        copy.wait()
    scatter(table, left, g, 12 * odd - 6, lambda j, p: offsets[0, j, p])

    @pl.when(odd == 0)
    def _():
        scatter(table, left, f, 6, lambda j, p: offsets[1, j, p])


def send(value, pairs):
    return lax.ppermute(value, AXES, pairs)


def after(*values):
    return lax.optimization_barrier(values)


def meta_scratch(count):
    return [
        pltpu.VMEM((count, META, TILE), jnp.int32),
        pltpu.SMEM((count, META, TILE), jnp.int32),
    ]


def shards(blocks, block_rows):
    count = lax.axis_size(AXES)
    device = lax.axis_index(AXES)
    columns = COLS * count
    devices = range(count)
    outward = [(s, (s + (2 if s % 2 else -2)) % count) for s in devices]
    inward = [(s, (s + (-2 if s % 2 else 2)) % count) for s in devices]
    onward = [(s, (s + (1 if s % 2 else -1)) % count) for s in devices]
    across = [(s, s ^ 1) for s in devices]

    mine = blocks.reshape(BODY, TILE)
    device = device.astype(jnp.int32).reshape(1)
    longer = call(
        functools.partial(pack_kernel, columns),
        pltpu.VMEM((LONG, TILE), BF16),
        [SMEM, HBM, HBM],
        VMEM,
        [
            pltpu.VMEM((COLS, SLOTS), jnp.int32),
            pltpu.VMEM((META, TILE), F32),
            pltpu.SemaphoreType.DMA((2,)),
        ],
        {},
        1,
        device,
        block_rows,
        mine,
    )
    packed = call(
        shorten_kernel,
        pltpu.VMEM((FULL, TILE), BF16),
        [VMEM],
        VMEM,
        [pltpu.SemaphoreType.DMA],
        {},
        1,
        longer,
    )
    x0 = send(packed, across)
    f = send(longer, outward)
    g = send(longer, inward)
    table = call(
        functools.partial(table_kernel, columns),
        jax.ShapeDtypeStruct((TABLE,), jnp.int32),
        [SMEM, SMEM],
        SMEM,
        [],
        {},
        2,
        device,
        block_rows,
    )
    left_shape = pltpu.VMEM((COLS * TALL, WIDE), BF16)
    total_shape = pltpu.VMEM((BODY, TILE), F32)
    out_shape = jax.ShapeDtypeStruct((BODY, TILE), BF16)
    left, total, right = call(
        own_kernel,
        (left_shape, total_shape, pltpu.VMEM((BODY, TILE), BF16)),
        [SMEM, VMEM],
        (VMEM, VMEM, VMEM),
        [],
        {},
        8,
        table,
        packed,
    )
    left, total = add_parts(table, left, total, right, (x0,), (3,), None, 0, 4)
    f, left = after(f, left)
    relay_shape = pltpu.VMEM((RELAY * TILE, TILE), BF16)
    relay, left = call(
        odd_kernel,
        (relay_shape, left_shape),
        [SMEM, VMEM, VMEM],
        (VMEM, VMEM),
        [
            pltpu.VMEM((META, TILE), jnp.int32),
            pltpu.SMEM((META, TILE), jnp.int32),
            pltpu.SemaphoreType.DMA,
        ],
        {2: 1},
        1,
        table,
        f,
        left,
    )
    g, left = after(g, left)
    joined = call(
        join_kernel,
        pltpu.VMEM((2 * LONG, TILE), BF16),
        [VMEM, VMEM],
        VMEM,
        [pltpu.SemaphoreType.DMA((2,))],
        {},
        1,
        f,
        g,
    )
    x = send(joined, across)
    relay, joined = after(relay, joined)
    relay = call(
        even_kernel,
        relay_shape,
        [SMEM, VMEM, VMEM],
        VMEM,
        [
            pltpu.VMEM((META, TILE), jnp.int32),
            pltpu.SMEM((META, TILE), jnp.int32),
            pltpu.SemaphoreType.DMA,
        ],
        {2: 0},
        1,
        device,
        f,
        relay,
    )
    relay = send(relay, onward)
    left = call(
        near_kernel,
        left_shape,
        [SMEM] + [VMEM] * 3,
        VMEM,
        [*meta_scratch(2), pltpu.SemaphoreType.DMA((2,))],
        {1: 0},
        4,
        table,
        left,
        f,
        g,
    )
    x, left = after(x, left)
    left, total, out = call(
        early_kernel,
        (left_shape, total_shape, out_shape),
        [SMEM] + [VMEM] * 4,
        (VMEM, VMEM, ANY),
        [
            *meta_scratch(2),
            pltpu.VMEM((WIDE, TILE), BF16),
            pltpu.VMEM((WIDE, TILE), BF16),
            pltpu.SemaphoreType.DMA((3,)),
        ],
        {1: 0, 2: 1},
        4,
        table,
        left,
        total,
        right,
        x,
    )
    out = call(
        last_kernel,
        (left_shape, total_shape, out_shape),
        [SMEM] + [VMEM] * 4 + [ANY],
        (VMEM, VMEM, ANY),
        [
            pltpu.VMEM((WIDE, TILE), BF16),
            pltpu.VMEM((2, WIDE, TILE), BF16),
            pltpu.SemaphoreType.DMA((2,)),
        ],
        {1: 0, 2: 1, 5: 2},
        4,
        table,
        left,
        total,
        right,
        relay,
        out,
    )[2]
    return out.reshape(COLS, SLOTS, TILE, TILE)


def solution(mesh):
    placed = (P(AXES, None, None, None), P(AXES, None))
    return jax.shard_map(
        shards,
        mesh=mesh,
        in_specs=placed,
        out_specs=P(AXES, None, None, None),
        check_vma=False,
    )
```

```python
import functools

import jax
import jax.numpy as jnp
from jax import lax
from jax.experimental import pallas as pl
from jax.experimental.pallas import tpu as pltpu
from jax.sharding import PartitionSpec as P

AXES = ("row", "col", "layer")
BAND = 8
TILE = 128
SLOTS = 12
COLS = 3
OWN = COLS * SLOTS
BODY = OWN * TILE
WIDE = SLOTS * TILE
META = 16
FULL = BODY + META
LONG = FULL + META
TALL = WIDE + TILE
FAR = BAND + 1
NEAR = BAND + 2
RELAY = FAR + NEAR
PLACE_AT = 0
ORDER_AT = PLACE_AT + OWN
SLOT_AT = ORDER_AT + OWN
SPAN = 40
SHIFT = 18
FIND_AT = SLOT_AT + OWN
STAGES = 3
TILES_AT = FIND_AT + COLS * SPAN
ODD_AT = TILES_AT + COLS * STAGES
TABLE = ODD_AT + 1
PAIR = 2 * TILE
PAIRS = SLOTS // 2
CHUNK = 256
GROUP = 4
BF16 = jnp.bfloat16
F32 = jnp.float32
ANY = pl.BlockSpec(memory_space=pl.ANY)
VMEM = pl.BlockSpec(memory_space=pltpu.VMEM)
HBM = pl.BlockSpec(memory_space=pltpu.HBM)
SMEM = pl.BlockSpec(memory_space=pltpu.SMEM)


def rows_at(start, size, unit=TILE):
    return pl.ds(pl.multiple_of(start, unit), size)


def call(kernel, out_shape, in_specs, out_specs, scratch, aliases, micros, *args):
    args = [
        pltpu.with_memory_space_constraint(arg, spec.memory_space)
        if spec in (VMEM, HBM) or arg.shape == (TABLE,)
        else arg
        for arg, spec in zip(args, in_specs)
    ]
    return pl.pallas_call(
        kernel,
        out_shape=out_shape,
        in_specs=in_specs,
        out_specs=out_specs,
        scratch_shapes=scratch,
        input_output_aliases=aliases,
        compiler_params=pltpu.CompilerParams(vmem_limit_bytes=16 * 2**20),
        cost_estimate=pl.CostEstimate(
            flops=0, bytes_accessed=int(micros * 3e6), transcendentals=0
        ),
    )(*args)


def wrapped(value, total):
    value = jnp.where(value >= total // 2, value - total, value)
    return jnp.where(value < -(total // 2), value + total, value)


def pack_kernel(total, device, rows, mine, longer, near_rows, wide, sem):
    body = pltpu.make_async_copy(mine, longer.at[pl.ds(0, BODY)], sem.at[0])
    lists = pltpu.make_async_copy(rows, near_rows, sem.at[1])
    body.start()
    lists.start()
    column = device[0] * COLS + lax.broadcasted_iota(jnp.int32, (COLS, SLOTS), 0)
    wide[...] = jnp.zeros_like(wide)
    longer[pl.ds(FULL, META), :] = jnp.zeros((META, TILE), BF16)
    lists.wait()
    wide[pl.ds(0, COLS), pl.ds(0, SLOTS)] = wrapped(near_rows[...] - column, total).astype(F32)
    longer[pl.ds(BODY, META), :] = wide[...].astype(BF16)
    body.wait()


def shorten_kernel(longer, packed, sem):
    copy = pltpu.make_async_copy(longer.at[pl.ds(0, FULL)], packed, sem)
    copy.start()
    copy.wait()


def table_kernel(total, device, rows, table):
    odd = device[0] % 2
    table[ODD_AT] = odd
    first = device[0] * COLS
    for c in range(COLS):
        for i in range(SPAN):
            table[FIND_AT + c * SPAN + i] = SLOTS
        places = [wrapped(rows[c, s] - first, total) for s in range(SLOTS)]
        keys, stages = [], []
        for s in range(SLOTS):
            group = (places[s] + BAND + 1) // COLS
            group = jnp.where(odd == 1, 6 - group, group)
            stage = jnp.where(group >= 3, jnp.maximum(group - 4, 0), group)
            stage = jnp.where(group == 0, 3, stage)
            stages.append(stage)
            keys.append(stage * 16 + s)
        for s in range(SLOTS):
            order = jnp.int32(0)
            for other in range(SLOTS):
                if other != s:
                    order = order + jnp.where(keys[other] < keys[s], 1, 0)
            table[PLACE_AT + c * SLOTS + s] = places[s]
            table[ORDER_AT + c * SLOTS + s] = order
            table[SLOT_AT + c * SLOTS + order] = s
            table[FIND_AT + c * SPAN + places[s] + SHIFT] = order
        for stage in range(STAGES):
            held = jnp.int32(0)
            for s in range(SLOTS):
                held = held + jnp.where(stages[s] <= stage, 1, 0)
            table[TILES_AT + c * STAGES + stage] = held // 2


def read_meta(packed, whole, offsets, sem):
    whole[...] = packed[pl.ds(BODY, META), :].astype(F32).astype(jnp.int32)
    copy = pltpu.make_async_copy(whole, offsets, sem)
    copy.start()
    return copy


def scatter(table, left, part, place, offset_at):
    for j in range(part.shape[0] // WIDE):
        for c in range(COLS):
            here = FIND_AT + c * SPAN + SHIFT + place + j
            k = table[here]

            @pl.when(k < SLOTS)
            def _():
                for start in range(0, SLOTS, GROUP):
                    taken = range(start, start + GROUP)
                    to = [table[here + offset_at(j, p)] for p in taken]
                    held = [part[rows_at((j * SLOTS + p) * TILE, TILE), :] for p in taken]
                    for s, block in zip(to, held):
                        left[
                            rows_at(c * TALL + s * TILE, TILE), rows_at(k * TILE, TILE)
                        ] = block


def accumulate(left, right, total, c, low, high):
    def one(t, carry):
        weights = right[rows_at(c * WIDE + t * PAIR, PAIR), :]
        for m in range(0, WIDE, CHUNK):
            here = rows_at(c * WIDE + m, CHUNK)
            total[here, :] += jnp.dot(
                left[rows_at(c * TALL + m, CHUNK), rows_at(t * PAIR, PAIR, PAIR)],
                weights,
                preferred_element_type=F32,
            )
        return carry

    lax.fori_loop(low, high, one, 0)


def tiles(table, c, stage):
    return table[TILES_AT + c * STAGES + stage]


def finish(table, left, total, c, square, result, out, sem):
    square[...] = total[rows_at(c * WIDE, WIDE), :].astype(BF16)
    for m in range(0, WIDE, CHUNK):
        cubed = jnp.dot(
            left[rows_at(c * TALL + m, CHUNK), :], square[...], preferred_element_type=F32
        )
        refined = (3.0 * square[pl.ds(m, CHUNK), :].astype(F32) - 2.0 * cubed).astype(BF16)
        for i in range(CHUNK // TILE):
            slot = table[SLOT_AT + c * SLOTS + m // TILE + i]
            here = rows_at(slot * TILE, TILE)
            result[here, :] = refined[i * TILE : (i + 1) * TILE]
            target = out.at[rows_at(c * WIDE + slot * TILE, TILE)]
            pltpu.make_async_copy(result.at[here], target, sem).start()
    return pltpu.make_async_copy(result, out.at[rows_at(c * WIDE, WIDE)], sem)


def own_kernel(table, mine, left, total, right):
    def clear(i, carry):
        left[rows_at(i * TILE, TILE), :] = jnp.zeros((TILE, WIDE), BF16)
        return carry

    lax.fori_loop(0, COLS * TALL // TILE, clear, 0)
    total[...] = jnp.zeros_like(total)

    def order(i, carry):
        c = i // SLOTS
        right[rows_at(c * WIDE + table[ORDER_AT + i] * TILE, TILE), :] = mine[
            rows_at(i * TILE, TILE), :
        ]
        return carry

    lax.fori_loop(0, OWN, order, 0)
    scatter(table, left, mine, 0, lambda j, p: table[PLACE_AT + j * SLOTS + p] - j)


def parts_kernel(places, low, high, table, left_in, total_in, right, *refs):
    del left_in, total_in
    parts, (left, total, whole, offsets, sem) = refs[: len(places)], refs[len(places) :]
    side = 1 - 2 * table[ODD_AT]
    copies = [
        read_meta(part, whole.at[i], offsets.at[i], sem.at[i]) for i, part in enumerate(parts)
    ]
    for i, (part, place) in enumerate(zip(parts, places)):
        copies[i].wait()
        scatter(table, left, part, place * side, lambda j, p: offsets[i, j, p])
    for c in range(COLS):
        accumulate(
            left, right, total, c, 0 if low is None else tiles(table, c, low), tiles(table, c, high)
        )


def add_parts(table, left, total, right, parts, places, low, high, micros):
    count = len(parts)
    return call(
        functools.partial(parts_kernel, places, low, high),
        (pltpu.VMEM(left.shape, BF16), pltpu.VMEM(total.shape, F32)),
        [SMEM] + [VMEM] * (3 + count),
        (VMEM, VMEM),
        [*meta_scratch(count), pltpu.SemaphoreType.DMA((count,))],
        {1: 0, 2: 1},
        micros,
        table,
        left,
        total,
        right,
        *parts,
    )


def early_kernel(
    table, left_in, total_in, right, x, left, total, out, whole, offsets, square, result, sem
):
    del left_in, total_in
    odd = table[ODD_AT]
    side = 1 - 2 * odd
    parts = [x.at[pl.ds(i * LONG, LONG)] for i in range(2)]
    copies = [
        read_meta(part, whole.at[i], offsets.at[i], sem.at[i]) for i, part in enumerate(parts)
    ]
    for c in range(COLS):
        accumulate(left, right, total, c, tiles(table, c, 0), tiles(table, c, 1))
    for i, (part, place) in enumerate(zip(parts, (-3, 9))):
        copies[i].wait()
        scatter(table, left, part, place * side, lambda j, p: offsets[i, j, p])
    first = 2 - 2 * odd
    accumulate(left, right, total, first, tiles(table, first, 1), PAIRS)
    copy = finish(table, left, total, first, square, result, out, sem.at[2])
    for c in (1, 2 * odd):
        accumulate(left, right, total, c, tiles(table, c, 1), tiles(table, c, 2))
    copy.wait()


def last_kernel(
    table, left_in, total_in, right, relay, out_in, left, total, out, square, result, sem
):
    del left_in, total_in, out_in
    odd = table[ODD_AT]
    copies = []
    for i, c in enumerate((1, 2 * odd)):
        for start, size, place, low in (
            (0, FAR, jnp.where(odd == 1, 10, -8), jnp.where(odd == 1, -8, 0)),
            (FAR, NEAR, jnp.where(odd == 1, 9, -7), jnp.where(odd == 1, -8, -1)),
        ):
            here = FIND_AT + c * SPAN + SHIFT + place
            k = table[here]

            @pl.when(k < SLOTS)
            def _():
                for p in range(size):
                    s = table[here + low + p]
                    left[
                        rows_at(c * TALL + s * TILE, TILE), rows_at(k * TILE, TILE)
                    ] = relay[pl.ds((start + p) * TILE, TILE), :]

        accumulate(left, right, total, c, tiles(table, c, 2), PAIRS)
        copies.append(finish(table, left, total, c, square, result.at[i], out, sem.at[i]))
    for copy in copies:
        copy.wait()


def fill_relay(odd, f, relay, offsets):
    relay[...] = jnp.zeros_like(relay)
    for column, start, size, shift in (
        (1, 0, FAR, 0 if odd else BAND),
        (2 * odd, FAR, NEAR, 1 if odd else BAND),
    ):

        def one(p, carry):
            at = offsets[column, p] + shift

            @pl.when((at >= 0) & (at < size))
            def _():
                relay[rows_at((start + at) * TILE, TILE), :] = f[
                    rows_at((column * SLOTS + p) * TILE, TILE), :
                ]

            return carry

        lax.fori_loop(0, SLOTS, one, 0)


def odd_kernel(table, f, left_in, relay, left, whole, offsets, sem):
    del left_in

    @pl.when(table[ODD_AT] == 1)
    def _():
        read_meta(f, whole, offsets, sem).wait()
        fill_relay(1, f, relay, offsets)
        scatter(table, left, f, -6, lambda j, p: offsets[j, p])


def even_kernel(device, f, relay_in, relay, whole, offsets, sem):
    del relay_in

    @pl.when(device[0] % 2 == 0)
    def _():
        read_meta(f, whole, offsets, sem).wait()
        fill_relay(0, f, relay, offsets)


def join_kernel(f, g, joined, sem):
    joins = [
        pltpu.make_async_copy(part, joined.at[pl.ds(i * LONG, LONG)], sem.at[i])
        for i, part in enumerate((f, g))
    ]
    for join in joins:
        join.start()
    for join in joins:
        join.wait()


def near_kernel(table, left_in, f, g, left, whole, offsets, sem):
    del left_in
    odd = table[ODD_AT]
    copies = [
        read_meta(part, whole.at[i], offsets.at[i], sem.at[i]) for i, part in enumerate((g, f))
    ]
    for copy in copies:
        copy.wait()
    scatter(table, left, g, 12 * odd - 6, lambda j, p: offsets[0, j, p])

    @pl.when(odd == 0)
    def _():
        scatter(table, left, f, 6, lambda j, p: offsets[1, j, p])


def send(value, pairs):
    return lax.ppermute(value, AXES, pairs)


def after(*values):
    return lax.optimization_barrier(values)


def meta_scratch(count):
    return [
        pltpu.VMEM((count, META, TILE), jnp.int32),
        pltpu.SMEM((count, META, TILE), jnp.int32),
    ]


def shards(blocks, block_rows):
    count = lax.axis_size(AXES)
    device = lax.axis_index(AXES)
    columns = COLS * count
    devices = range(count)
    outward = [(s, (s + (2 if s % 2 else -2)) % count) for s in devices]
    inward = [(s, (s + (-2 if s % 2 else 2)) % count) for s in devices]
    onward = [(s, (s + (1 if s % 2 else -1)) % count) for s in devices]
    across = [(s, s ^ 1) for s in devices]

    mine = blocks.reshape(BODY, TILE)
    device = device.astype(jnp.int32).reshape(1)
    longer = call(
        functools.partial(pack_kernel, columns),
        pltpu.VMEM((LONG, TILE), BF16),
        [SMEM, HBM, HBM],
        VMEM,
        [
            pltpu.VMEM((COLS, SLOTS), jnp.int32),
            pltpu.VMEM((META, TILE), F32),
            pltpu.SemaphoreType.DMA((2,)),
        ],
        {},
        1,
        device,
        block_rows,
        mine,
    )
    packed = call(
        shorten_kernel,
        pltpu.VMEM((FULL, TILE), BF16),
        [VMEM],
        VMEM,
        [pltpu.SemaphoreType.DMA],
        {},
        1,
        longer,
    )
    x0 = send(packed, across)
    f = send(longer, outward)
    g = send(longer, inward)
    table = call(
        functools.partial(table_kernel, columns),
        pltpu.SMEM((TABLE,), jnp.int32),
        [SMEM, SMEM],
        SMEM,
        [],
        {},
        2,
        device,
        block_rows,
    )
    left_shape = pltpu.VMEM((COLS * TALL, WIDE), BF16)
    total_shape = pltpu.VMEM((BODY, TILE), F32)
    out_shape = jax.ShapeDtypeStruct((BODY, TILE), BF16)
    left, total, right = call(
        own_kernel,
        (left_shape, total_shape, pltpu.VMEM((BODY, TILE), BF16)),
        [SMEM, VMEM],
        (VMEM, VMEM, VMEM),
        [],
        {},
        8,
        table,
        packed,
    )
    left, total = add_parts(table, left, total, right, (x0,), (3,), None, 0, 4)
    f, left = after(f, left)
    relay_shape = pltpu.VMEM((RELAY * TILE, TILE), BF16)
    relay, left = call(
        odd_kernel,
        (relay_shape, left_shape),
        [SMEM, VMEM, VMEM],
        (VMEM, VMEM),
        [
            pltpu.VMEM((META, TILE), jnp.int32),
            pltpu.SMEM((META, TILE), jnp.int32),
            pltpu.SemaphoreType.DMA,
        ],
        {2: 1},
        1,
        table,
        f,
        left,
    )
    g, left = after(g, left)
    joined = call(
        join_kernel,
        pltpu.VMEM((2 * LONG, TILE), BF16),
        [VMEM, VMEM],
        VMEM,
        [pltpu.SemaphoreType.DMA((2,))],
        {},
        1,
        f,
        g,
    )
    x = send(joined, across)
    relay, joined = after(relay, joined)
    relay = call(
        even_kernel,
        relay_shape,
        [SMEM, VMEM, VMEM],
        VMEM,
        [
            pltpu.VMEM((META, TILE), jnp.int32),
            pltpu.SMEM((META, TILE), jnp.int32),
            pltpu.SemaphoreType.DMA,
        ],
        {2: 0},
        1,
        device,
        f,
        relay,
    )
    relay = send(relay, onward)
    left = call(
        near_kernel,
        left_shape,
        [SMEM] + [VMEM] * 3,
        VMEM,
        [*meta_scratch(2), pltpu.SemaphoreType.DMA((2,))],
        {1: 0},
        4,
        table,
        left,
        f,
        g,
    )
    x, left = after(x, left)
    left, total, out = call(
        early_kernel,
        (left_shape, total_shape, out_shape),
        [SMEM] + [VMEM] * 4,
        (VMEM, VMEM, ANY),
        [
            *meta_scratch(2),
            pltpu.VMEM((WIDE, TILE), BF16),
            pltpu.VMEM((WIDE, TILE), BF16),
            pltpu.SemaphoreType.DMA((3,)),
        ],
        {1: 0, 2: 1},
        4,
        table,
        left,
        total,
        right,
        x,
    )
    out = call(
        last_kernel,
        (left_shape, total_shape, out_shape),
        [SMEM] + [VMEM] * 4 + [ANY],
        (VMEM, VMEM, ANY),
        [
            pltpu.VMEM((WIDE, TILE), BF16),
            pltpu.VMEM((2, WIDE, TILE), BF16),
            pltpu.SemaphoreType.DMA((2,)),
        ],
        {1: 0, 2: 1, 5: 2},
        4,
        table,
        left,
        total,
        right,
        relay,
        out,
    )[2]
    return out.reshape(COLS, SLOTS, TILE, TILE)


def solution(mesh):
    placed = (P(AXES, None, None, None), P(AXES, None))
    return jax.shard_map(
        shards,
        mesh=mesh,
        in_specs=placed,
        out_specs=P(AXES, None, None, None),
        check_vma=False,
    )
```

```python
import functools

import jax
import jax.numpy as jnp
from jax import lax
from jax.experimental import pallas as pl
from jax.experimental.pallas import tpu as pltpu
from jax.sharding import PartitionSpec as P

AXES = ("row", "col", "layer")
BAND = 8
TILE = 128
SLOTS = 12
COLS = 3
OWN = COLS * SLOTS
BODY = OWN * TILE
WIDE = SLOTS * TILE
META = 16
FULL = BODY + META
LONG = FULL + META
TALL = WIDE + TILE
FAR = BAND + 1
NEAR = BAND + 2
RELAY = FAR + NEAR
PLACE_AT = 0
ORDER_AT = PLACE_AT + OWN
SLOT_AT = ORDER_AT + OWN
SPAN = 40
SHIFT = 18
FIND_AT = SLOT_AT + OWN
STAGES = 3
TILES_AT = FIND_AT + COLS * SPAN
ODD_AT = TILES_AT + COLS * STAGES
TABLE = ODD_AT + 1
PAIR = 2 * TILE
PAIRS = SLOTS // 2
CHUNK = 256
GROUP = 4
BF16 = jnp.bfloat16
F32 = jnp.float32
ANY = pl.BlockSpec(memory_space=pl.ANY)
VMEM = pl.BlockSpec(memory_space=pltpu.VMEM)
HBM = pl.BlockSpec(memory_space=pltpu.HBM)
SMEM = pl.BlockSpec(memory_space=pltpu.SMEM)


def rows_at(start, size, unit=TILE):
    return pl.ds(pl.multiple_of(start, unit), size)


def call(kernel, out_shape, in_specs, out_specs, scratch, aliases, micros, *args):
    args = [
        pltpu.with_memory_space_constraint(arg, spec.memory_space)
        if spec in (VMEM, HBM) or arg.shape == (TABLE,)
        else arg
        for arg, spec in zip(args, in_specs)
    ]
    return pl.pallas_call(
        kernel,
        out_shape=out_shape,
        in_specs=in_specs,
        out_specs=out_specs,
        scratch_shapes=scratch,
        input_output_aliases=aliases,
        compiler_params=pltpu.CompilerParams(vmem_limit_bytes=16 * 2**20),
        cost_estimate=pl.CostEstimate(
            flops=0, bytes_accessed=int(micros * 3e6), transcendentals=0
        ),
    )(*args)


def wrapped(value, total):
    value = jnp.where(value >= total // 2, value - total, value)
    return jnp.where(value < -(total // 2), value + total, value)


def pack_kernel(total, device, rows, mine, longer, near_rows, wide, sem):
    lists = pltpu.make_async_copy(rows, near_rows, sem.at[0])
    lists.start()
    pieces = [
        pltpu.make_async_copy(
            mine.at[pl.ds(i * BODY // 4, BODY // 4)],
            longer.at[pl.ds(i * BODY // 4, BODY // 4)],
            sem.at[1 + i],
        )
        for i in range(4)
    ]
    for piece in pieces:
        piece.start()
    column = device[0] * COLS + lax.broadcasted_iota(jnp.int32, (COLS, SLOTS), 0)
    wide[...] = jnp.zeros_like(wide)
    longer[pl.ds(FULL, META), :] = jnp.zeros((META, TILE), BF16)
    lists.wait()
    wide[pl.ds(0, COLS), pl.ds(0, SLOTS)] = wrapped(near_rows[...] - column, total).astype(F32)
    longer[pl.ds(BODY, META), :] = wide[...].astype(BF16)
    for piece in pieces:
        piece.wait()


def shorten_kernel(longer, packed, sem):
    copy = pltpu.make_async_copy(longer.at[pl.ds(0, FULL)], packed, sem)
    copy.start()
    copy.wait()


def table_kernel(total, device, rows, table):
    odd = device[0] % 2
    table[ODD_AT] = odd
    first = device[0] * COLS
    for c in range(COLS):
        for i in range(SPAN):
            table[FIND_AT + c * SPAN + i] = SLOTS
        places = [wrapped(rows[c, s] - first, total) for s in range(SLOTS)]
        keys, stages = [], []
        for s in range(SLOTS):
            group = (places[s] + BAND + 1) // COLS
            group = jnp.where(odd == 1, 6 - group, group)
            stage = jnp.where(group >= 3, jnp.maximum(group - 4, 0), group)
            stage = jnp.where(group == 0, 3, stage)
            stages.append(stage)
            keys.append(stage * 16 + s)
        for s in range(SLOTS):
            order = jnp.int32(0)
            for other in range(SLOTS):
                if other != s:
                    order = order + jnp.where(keys[other] < keys[s], 1, 0)
            table[PLACE_AT + c * SLOTS + s] = places[s]
            table[ORDER_AT + c * SLOTS + s] = order
            table[SLOT_AT + c * SLOTS + order] = s
            table[FIND_AT + c * SPAN + places[s] + SHIFT] = order
        for stage in range(STAGES):
            held = jnp.int32(0)
            for s in range(SLOTS):
                held = held + jnp.where(stages[s] <= stage, 1, 0)
            table[TILES_AT + c * STAGES + stage] = held // 2


def read_meta(packed, whole, offsets, sem):
    whole[...] = packed[pl.ds(BODY, META), :].astype(F32).astype(jnp.int32)
    copy = pltpu.make_async_copy(whole, offsets, sem)
    copy.start()
    return copy


def scatter(table, left, part, place, offset_at):
    for j in range(part.shape[0] // WIDE):
        for c in range(COLS):
            here = FIND_AT + c * SPAN + SHIFT + place + j
            k = table[here]

            @pl.when(k < SLOTS)
            def _():
                for start in range(0, SLOTS, GROUP):
                    taken = range(start, start + GROUP)
                    to = [table[here + offset_at(j, p)] for p in taken]
                    held = [part[rows_at((j * SLOTS + p) * TILE, TILE), :] for p in taken]
                    for s, block in zip(to, held):
                        left[
                            rows_at(c * TALL + s * TILE, TILE), rows_at(k * TILE, TILE)
                        ] = block


def accumulate(left, right, total, c, low, high):
    def one(t, carry):
        weights = right[rows_at(c * WIDE + t * PAIR, PAIR), :]
        for m in range(0, WIDE, CHUNK):
            here = rows_at(c * WIDE + m, CHUNK)
            total[here, :] += jnp.dot(
                left[rows_at(c * TALL + m, CHUNK), rows_at(t * PAIR, PAIR, PAIR)],
                weights,
                preferred_element_type=F32,
            )
        return carry

    lax.fori_loop(low, high, one, 0)


def tiles(table, c, stage):
    return table[TILES_AT + c * STAGES + stage]


def finish(table, left, total, c, square, result, out, sem):
    square[...] = total[rows_at(c * WIDE, WIDE), :].astype(BF16)
    for m in range(0, WIDE, CHUNK):
        cubed = jnp.dot(
            left[rows_at(c * TALL + m, CHUNK), :], square[...], preferred_element_type=F32
        )
        refined = (3.0 * square[pl.ds(m, CHUNK), :].astype(F32) - 2.0 * cubed).astype(BF16)
        for i in range(CHUNK // TILE):
            slot = table[SLOT_AT + c * SLOTS + m // TILE + i]
            here = rows_at(slot * TILE, TILE)
            result[here, :] = refined[i * TILE : (i + 1) * TILE]
            target = out.at[rows_at(c * WIDE + slot * TILE, TILE)]
            pltpu.make_async_copy(result.at[here], target, sem).start()
    return pltpu.make_async_copy(result, out.at[rows_at(c * WIDE, WIDE)], sem)


def own_kernel(table, mine, left, total, right):
    def clear(i, carry):
        left[rows_at(i * TILE, TILE), :] = jnp.zeros((TILE, WIDE), BF16)
        return carry

    lax.fori_loop(0, COLS * TALL // TILE, clear, 0)
    total[...] = jnp.zeros_like(total)

    def order(i, carry):
        c = i // SLOTS
        right[rows_at(c * WIDE + table[ORDER_AT + i] * TILE, TILE), :] = mine[
            rows_at(i * TILE, TILE), :
        ]
        return carry

    lax.fori_loop(0, OWN, order, 0)
    scatter(table, left, mine, 0, lambda j, p: table[PLACE_AT + j * SLOTS + p] - j)


def parts_kernel(places, low, high, table, left_in, total_in, right, *refs):
    del left_in, total_in
    parts, (left, total, whole, offsets, sem) = refs[: len(places)], refs[len(places) :]
    side = 1 - 2 * table[ODD_AT]
    copies = [
        read_meta(part, whole.at[i], offsets.at[i], sem.at[i]) for i, part in enumerate(parts)
    ]
    for i, (part, place) in enumerate(zip(parts, places)):
        copies[i].wait()
        scatter(table, left, part, place * side, lambda j, p: offsets[i, j, p])
    for c in range(COLS):
        accumulate(
            left, right, total, c, 0 if low is None else tiles(table, c, low), tiles(table, c, high)
        )


def add_parts(table, left, total, right, parts, places, low, high, micros):
    count = len(parts)
    return call(
        functools.partial(parts_kernel, places, low, high),
        (pltpu.VMEM(left.shape, BF16), pltpu.VMEM(total.shape, F32)),
        [SMEM] + [VMEM] * (3 + count),
        (VMEM, VMEM),
        [*meta_scratch(count), pltpu.SemaphoreType.DMA((count,))],
        {1: 0, 2: 1},
        micros,
        table,
        left,
        total,
        right,
        *parts,
    )


def early_kernel(
    table, left_in, total_in, right, x, left, total, out, whole, offsets, square, result, sem
):
    del left_in, total_in
    odd = table[ODD_AT]
    side = 1 - 2 * odd
    parts = [x.at[pl.ds(i * LONG, LONG)] for i in range(2)]
    copies = [
        read_meta(part, whole.at[i], offsets.at[i], sem.at[i]) for i, part in enumerate(parts)
    ]
    for c in range(COLS):
        accumulate(left, right, total, c, tiles(table, c, 0), tiles(table, c, 1))
    for i, (part, place) in enumerate(zip(parts, (-3, 9))):
        copies[i].wait()
        scatter(table, left, part, place * side, lambda j, p: offsets[i, j, p])
    first = 2 - 2 * odd
    accumulate(left, right, total, first, tiles(table, first, 1), PAIRS)
    copy = finish(table, left, total, first, square, result, out, sem.at[2])
    for c in (1, 2 * odd):
        accumulate(left, right, total, c, tiles(table, c, 1), tiles(table, c, 2))
    copy.wait()


def last_kernel(
    table, left_in, total_in, right, relay, out_in, left, total, out, square, result, sem
):
    del left_in, total_in, out_in
    odd = table[ODD_AT]
    copies = []
    for i, c in enumerate((1, 2 * odd)):
        for start, size, place, low in (
            (0, FAR, jnp.where(odd == 1, 10, -8), jnp.where(odd == 1, -8, 0)),
            (FAR, NEAR, jnp.where(odd == 1, 9, -7), jnp.where(odd == 1, -8, -1)),
        ):
            here = FIND_AT + c * SPAN + SHIFT + place
            k = table[here]

            @pl.when(k < SLOTS)
            def _():
                for p in range(size):
                    s = table[here + low + p]
                    left[
                        rows_at(c * TALL + s * TILE, TILE), rows_at(k * TILE, TILE)
                    ] = relay[pl.ds((start + p) * TILE, TILE), :]

        accumulate(left, right, total, c, tiles(table, c, 2), PAIRS)
        copies.append(finish(table, left, total, c, square, result.at[i], out, sem.at[i]))
    for copy in copies:
        copy.wait()


def fill_relay(odd, f, relay, offsets):
    for column, start, size, shift in (
        (1, 0, FAR, 0 if odd else BAND),
        (2 * odd, FAR, NEAR, 1 if odd else BAND),
    ):

        def one(p, carry):
            at = offsets[column, p] + shift

            @pl.when((at >= 0) & (at < size))
            def _():
                relay[rows_at((start + at) * TILE, TILE), :] = f[
                    rows_at((column * SLOTS + p) * TILE, TILE), :
                ]

            return carry

        lax.fori_loop(0, SLOTS, one, 0)


def odd_kernel(table, f, left_in, relay, left, whole, offsets, sem):
    del left_in

    @pl.when(table[ODD_AT] == 1)
    def _():
        copy = read_meta(f, whole, offsets, sem)
        relay[...] = jnp.zeros_like(relay)
        copy.wait()
        fill_relay(1, f, relay, offsets)
        scatter(table, left, f, -6, lambda j, p: offsets[j, p])


def even_kernel(device, f, relay_in, relay, whole, offsets, sem):
    del relay_in

    @pl.when(device[0] % 2 == 0)
    def _():
        copy = read_meta(f, whole, offsets, sem)
        relay[...] = jnp.zeros_like(relay)
        copy.wait()
        fill_relay(0, f, relay, offsets)


def join_kernel(f, g, joined, sem):
    joins = [
        pltpu.make_async_copy(part, joined.at[pl.ds(i * LONG, LONG)], sem.at[i])
        for i, part in enumerate((f, g))
    ]
    for join in joins:
        join.start()
    for join in joins:
        join.wait()


def near_kernel(table, left_in, f, g, left, whole, offsets, sem):
    del left_in
    odd = table[ODD_AT]
    copies = [
        read_meta(part, whole.at[i], offsets.at[i], sem.at[i]) for i, part in enumerate((g, f))
    ]
    for copy in copies:
        copy.wait()
    scatter(table, left, g, 12 * odd - 6, lambda j, p: offsets[0, j, p])

    @pl.when(odd == 0)
    def _():
        scatter(table, left, f, 6, lambda j, p: offsets[1, j, p])


def send(value, pairs):
    return lax.ppermute(value, AXES, pairs)


def after(*values):
    return lax.optimization_barrier(values)


def meta_scratch(count):
    return [
        pltpu.VMEM((count, META, TILE), jnp.int32),
        pltpu.SMEM((count, META, TILE), jnp.int32),
    ]


def shards(blocks, block_rows):
    count = lax.axis_size(AXES)
    device = lax.axis_index(AXES)
    columns = COLS * count
    devices = range(count)
    outward = [(s, (s + (2 if s % 2 else -2)) % count) for s in devices]
    inward = [(s, (s + (-2 if s % 2 else 2)) % count) for s in devices]
    onward = [(s, (s + (1 if s % 2 else -1)) % count) for s in devices]
    across = [(s, s ^ 1) for s in devices]

    mine = blocks.reshape(BODY, TILE)
    device = device.astype(jnp.int32).reshape(1)
    longer = call(
        functools.partial(pack_kernel, columns),
        pltpu.VMEM((LONG, TILE), BF16),
        [SMEM, HBM, HBM],
        VMEM,
        [
            pltpu.VMEM((COLS, SLOTS), jnp.int32),
            pltpu.VMEM((META, TILE), F32),
            pltpu.SemaphoreType.DMA((5,)),
        ],
        {},
        1,
        device,
        block_rows,
        mine,
    )
    packed = call(
        shorten_kernel,
        pltpu.VMEM((FULL, TILE), BF16),
        [VMEM],
        VMEM,
        [pltpu.SemaphoreType.DMA],
        {},
        1,
        longer,
    )
    x0 = send(packed, across)
    f = send(longer, outward)
    g = send(longer, inward)
    table = call(
        functools.partial(table_kernel, columns),
        pltpu.SMEM((TABLE,), jnp.int32),
        [SMEM, SMEM],
        SMEM,
        [],
        {},
        2,
        device,
        block_rows,
    )
    left_shape = pltpu.VMEM((COLS * TALL, WIDE), BF16)
    total_shape = pltpu.VMEM((BODY, TILE), F32)
    out_shape = jax.ShapeDtypeStruct((BODY, TILE), BF16)
    left, total, right = call(
        own_kernel,
        (left_shape, total_shape, pltpu.VMEM((BODY, TILE), BF16)),
        [SMEM, VMEM],
        (VMEM, VMEM, VMEM),
        [],
        {},
        8,
        table,
        packed,
    )
    left, total = add_parts(table, left, total, right, (x0,), (3,), None, 0, 4)
    f, left = after(f, left)
    relay_shape = pltpu.VMEM((RELAY * TILE, TILE), BF16)
    relay, left = call(
        odd_kernel,
        (relay_shape, left_shape),
        [SMEM, VMEM, VMEM],
        (VMEM, VMEM),
        [
            pltpu.VMEM((META, TILE), jnp.int32),
            pltpu.SMEM((META, TILE), jnp.int32),
            pltpu.SemaphoreType.DMA,
        ],
        {2: 1},
        1,
        table,
        f,
        left,
    )
    g, left = after(g, left)
    joined = call(
        join_kernel,
        pltpu.VMEM((2 * LONG, TILE), BF16),
        [VMEM, VMEM],
        VMEM,
        [pltpu.SemaphoreType.DMA((2,))],
        {},
        1,
        f,
        g,
    )
    x = send(joined, across)
    relay, joined = after(relay, joined)
    relay = call(
        even_kernel,
        relay_shape,
        [SMEM, VMEM, VMEM],
        VMEM,
        [
            pltpu.VMEM((META, TILE), jnp.int32),
            pltpu.SMEM((META, TILE), jnp.int32),
            pltpu.SemaphoreType.DMA,
        ],
        {2: 0},
        1,
        device,
        f,
        relay,
    )
    relay = send(relay, onward)
    left = call(
        near_kernel,
        left_shape,
        [SMEM] + [VMEM] * 3,
        VMEM,
        [*meta_scratch(2), pltpu.SemaphoreType.DMA((2,))],
        {1: 0},
        4,
        table,
        left,
        f,
        g,
    )
    x, left = after(x, left)
    left, total, out = call(
        early_kernel,
        (left_shape, total_shape, out_shape),
        [SMEM] + [VMEM] * 4,
        (VMEM, VMEM, ANY),
        [
            *meta_scratch(2),
            pltpu.VMEM((WIDE, TILE), BF16),
            pltpu.VMEM((WIDE, TILE), BF16),
            pltpu.SemaphoreType.DMA((3,)),
        ],
        {1: 0, 2: 1},
        4,
        table,
        left,
        total,
        right,
        x,
    )
    out = call(
        last_kernel,
        (left_shape, total_shape, out_shape),
        [SMEM] + [VMEM] * 4 + [ANY],
        (VMEM, VMEM, ANY),
        [
            pltpu.VMEM((WIDE, TILE), BF16),
            pltpu.VMEM((2, WIDE, TILE), BF16),
            pltpu.SemaphoreType.DMA((2,)),
        ],
        {1: 0, 2: 1, 5: 2},
        4,
        table,
        left,
        total,
        right,
        relay,
        out,
    )[2]
    return out.reshape(COLS, SLOTS, TILE, TILE)


def solution(mesh):
    placed = (P(AXES, None, None, None), P(AXES, None))
    return jax.shard_map(
        shards,
        mesh=mesh,
        in_specs=placed,
        out_specs=P(AXES, None, None, None),
        check_vma=False,
    )
```
